32 devices in a mesh: grp: 2 (over x), blk: 16 (over z, y, core).
Axes of the slice: x: 2, y: 2, z: 4, core: 2. Of those that a mesh axis runs over, the one named last changes fastest.
Arguments:
- heads: float32 [8192, 768], P(('grp', 'blk')), parts along dimension 0, may hold values from -1.5 to 1.5
- head_state: float32 [8192], P(('grp', 'blk')), parts along dimension 0, may hold values from 0.005 to 0.2
- tails: float32 [16384, 768], P(('grp', 'blk')), parts along dimension 0, may hold values from -1.5 to 1.5
- tail_state: float32 [16384], P(('grp', 'blk')), parts along dimension 0, may hold values from 0.005 to 0.2
- relation: float32 [1536, 768], P(('grp', 'blk')), parts along dimension 0, may hold values from -0.21875 to 0.21875
- relation_state: float32 [1536], P(('grp', 'blk')), parts along dimension 0, may hold values from 50 to 2000
- pos_head: int32 [2, 16384], P(None, ('grp', 'blk')), parts along dimension 1, may hold values from 0 to 255
- pos_tail: int32 [2, 16384], P(None, ('grp', 'blk')), parts along dimension 1, may hold values from 0 to 511
Outputs:
- heads_out: float32 [8192, 768], P(('grp', 'blk')), parts along dimension 0
- head_state_out: float32 [8192], P(('grp', 'blk')), parts along dimension 0
- tails_out: float32 [16384, 768], P(('grp', 'blk')), parts along dimension 0
- tail_state_out: float32 [16384], P(('grp', 'blk')), parts along dimension 0
- relation_out: float32 [1536, 768], P(('grp', 'blk')), parts along dimension 0
- relation_state_out: float32 [1536], P(('grp', 'blk')), parts along dimension 0
The draws below stay inside these ranges and needn't reach their ends.
There are 2 independent parts, one for each index of `grp`. The reference program is written for one: setup_inputs(seed, part) draws one part's arguments, and reference() takes and returns one part's arrays. A program takes and returns all parts, laid end to end along the dimension named above; each array names one. Nothing has to cross between parts.
All inputs are finite; a program needn't handle non-finite values.
Results may differ from the reference program's by a relative error of at most 0.0003.
Values sent between devices are 32-bit elements; how exact they have to be, the bound alone decides.
No kernel may reach another device: no remote copies, remote signals or barrier semaphores. Data moves between devices by JAX's collectives and lax.ppermute only.
A program may use at most 64 MiB of HBM per device.

```python
import math
import jax
import jax.numpy as jnp
from jax import lax

D = 768
HEAD_ROWS = 256
TAIL_ROWS = 512
POS = 512
HEADS = 4096
TAILS = 8192
PAIRS = 8192
N_BLK = 16


def set_ends(entries, rng, least, high):
    dims = entries.shape
    spot = [jax.random.randint(jax.random.fold_in(rng, axis), (), 0, dims[axis]) for axis in range(len(dims))]
    entries = entries.at[tuple(spot)].set(least)
    longest = dims.index(max(dims))
    spot[longest] = (spot[longest] + 1) % dims[longest]
    return entries.at[tuple(spot)].set(high)


def level_of(rng, shape, shards, low, largest):
    def one(position, parts):
        draws = jax.random.uniform(jax.random.fold_in(jax.random.fold_in(rng, 6), position), (parts,), jnp.float32, low / len(shards), largest / len(shards))
        return jnp.repeat(jnp.exp(draws), shape[position] // parts).reshape((-1,) + (1,) * (len(shape) - position - 1))

    factor_of = one(*shards[0])
    for cut in shards[1:]:
        factor_of = factor_of * one(*cut)
    return factor_of


def scatter_about(own_key, extent, deviation, limit, cuts=(), held_as=jnp.bfloat16):
    gain = level_of(own_key, extent, cuts, -0.22, 0.18) if cuts else 1.0
    array = jax.random.normal(own_key, extent, jnp.float32) * deviation * gain
    return jnp.minimum(jnp.maximum(array, -limit), limit).astype(held_as)


def setup_inputs(seed: int = 0, part: int = 0) -> dict:
    seeds = jax.random.split(jax.random.key(seed), 9)
    own_keys = jax.random.split(jax.random.fold_in(seeds[8], part), 9)
    heads = scatter_about(own_keys[0], (HEADS, D), 0.25, 1.5, ((0, 16),), jnp.float32)
    head_state = jnp.clip(jnp.exp(math.log(0.2) - 3.6888795 * jax.random.uniform(own_keys[1], (HEADS,), jnp.float32) ** level_of(own_keys[1], (HEADS,), ((0, 16),), -0.2, 0.2)), 0.005, 0.2)
    tails = scatter_about(own_keys[2], (TAILS, D), 0.25, 1.5, ((0, 16),), jnp.float32)
    tail_state = jnp.clip(jnp.exp(math.log(0.2) - 3.6888795 * jax.random.uniform(own_keys[3], (TAILS,), jnp.float32) ** level_of(own_keys[3], (TAILS,), ((0, 16),), -0.2, 0.2)), 0.005, 0.2)
    relation = scatter_about(own_keys[4], (D, D), D ** -0.5, 0.21875, ((0, 16),), jnp.float32)
    relation_state = jnp.clip(jnp.exp(math.log(2000.0) - 3.6888795 * jax.random.uniform(own_keys[5], (D,), jnp.float32) ** level_of(own_keys[5], (D,), ((0, 16),), -0.2, 0.2)), 50.0, 2000.0)
    pos_head = set_ends(jax.random.randint(own_keys[6], (2, PAIRS), 0, HEAD_ROWS), jax.random.fold_in(own_keys[6], 1), 0, HEAD_ROWS - 1).astype(jnp.int32)
    pos_tail = set_ends(jax.random.randint(own_keys[7], (2, PAIRS), 0, TAIL_ROWS), jax.random.fold_in(own_keys[7], 1), 0, TAIL_ROWS - 1).astype(jnp.int32)
    return {"heads": heads, "head_state": head_state, "tails": tails, "tail_state": tail_state, "relation": relation, "relation_state": relation_state, "pos_head": pos_head, "pos_tail": pos_tail}


HIGH = lax.Precision.HIGHEST

def row_adagrad(param, state, grad):
    new_state = state + lax.optimization_barrier(jnp.mean(grad * grad, axis=-1))
    return (param - 0.1 * grad / jnp.sqrt(new_state)[:, None], new_state)

def positives_table(head_idx, tail_idx, head_rows, tail_rows):
    onehot_heads = (head_idx[:, None] == jnp.arange(head_rows, dtype=jnp.int32)[None, :]).astype(jnp.bfloat16)
    onehot_tails = (tail_idx[:, None] == jnp.arange(tail_rows, dtype=jnp.int32)[None, :]).astype(jnp.bfloat16)
    return lax.dot_general(onehot_heads, onehot_tails, (((0,), (0,)), ((), ())), preferred_element_type=jnp.float32)

def tile_grads(product, tail_block, head_idx, tail_idx):
    scores = lax.dot_general(product, tail_block, (((1,), (1,)), ((), ())), precision=HIGH, preferred_element_type=jnp.float32)
    marks = positives_table(head_idx, tail_idx, product.shape[0], tail_block.shape[0]).astype(scores.dtype)
    grad_scores = (jax.nn.sigmoid(scores) - marks) * 0.0625
    grad_tails = lax.dot_general(grad_scores, product, (((0,), (0,)), ((), ())), precision=HIGH, preferred_element_type=jnp.float32)
    grad_product = jnp.dot(grad_scores, tail_block, precision=HIGH, preferred_element_type=jnp.float32)
    return (grad_tails, grad_product)

def reference(heads, head_state, tails, tail_state, relation, relation_state, pos_head, pos_tail):
    for bucket in range(2):
        if bucket == 1:
            tails = jnp.roll(tails, TAIL_ROWS, axis=0)
            tail_state = jnp.roll(tail_state, TAIL_ROWS, axis=0)
        product = jnp.dot(heads, relation, precision=HIGH, preferred_element_type=jnp.float32)
        blocks = (product.reshape(N_BLK, HEAD_ROWS, D), tails.reshape(N_BLK, TAIL_ROWS, D), pos_head[bucket].reshape(N_BLK, POS), pos_tail[bucket].reshape(N_BLK, POS))

        def one_block(items):
            return tile_grads(items[0], items[1], items[2], items[3])
        grad_tails, grad_product = lax.map(one_block, blocks)
        grad_tails = grad_tails.reshape(TAILS, D)
        grad_product = grad_product.reshape(HEADS, D)
        grad_heads = lax.dot_general(grad_product, relation, (((1,), (1,)), ((), ())), precision=HIGH, preferred_element_type=jnp.float32)
        grad_relation = lax.dot_general(heads, grad_product, (((0,), (0,)), ((), ())), precision=HIGH, preferred_element_type=jnp.float32)
        tails, tail_state = row_adagrad(tails, tail_state, grad_tails)
        heads, head_state = row_adagrad(heads, head_state, grad_heads)
        relation, relation_state = row_adagrad(relation, relation_state, grad_relation)
    return (heads, head_state, tails, tail_state, relation, relation_state)
```

```python
import functools

import jax
import jax.numpy as jnp
from jax import lax
from jax.experimental import pallas as pl
from jax.experimental.pallas import tpu as pltpu
from jax.sharding import PartitionSpec as P

F32 = jnp.float32
BF16 = jnp.bfloat16
NN = (((1,), (0,)), ((), ()))
NT = (((1,), (1,)), ((), ()))
VMEM = pl.BlockSpec(memory_space=pltpu.VMEM)
SMEM = pl.BlockSpec(memory_space=pltpu.SMEM)


def split(x):
    high = x.astype(BF16)
    return high, (x - high.astype(F32)).astype(BF16)


def dot3(a, b, dims):
    def one(p, q):
        return lax.dot_general(p, q, dims, preferred_element_type=F32)

    return one(a[0], b[0]) + (one(a[0], b[1]) + one(a[1], b[0]))


def diagonal(n):
    return lax.broadcasted_iota(jnp.int32, (n, n), 0) == lax.broadcasted_iota(jnp.int32, (n, n), 1)


def adagrad(param, state_row, grad):
    n = param.shape[0]
    eye = diagonal(n)
    state = jnp.sum(jnp.where(eye, state_row, 0.0), axis=1, keepdims=True)
    state = state + jnp.sum(grad * grad, axis=1, keepdims=True) * (1.0 / grad.shape[1])
    back = jnp.sum(jnp.where(eye, state, 0.0), axis=0, keepdims=True)
    return param - grad * (0.1 / jnp.sqrt(state)), back


def to_slots(me, source, target, slots):
    rows = source.shape[0] // slots
    for r in range(slots):
        start = pl.multiple_of((me ^ r) * rows, rows)
        target[r * rows : (r + 1) * rows, :] = source[pl.ds(start, rows), :]


def from_slots(me, source, target, slots):
    rows = source.shape[0] // slots
    for r in range(slots):
        start = pl.multiple_of((me ^ r) * rows, rows)
        target[pl.ds(start, rows), :] = source[r * rows : (r + 1) * rows, :]


def write_head_parts(me, heads, outs, normal, slotted, slots):
    normal[...] = heads.T
    to_slots(me, normal, slotted, slots)
    turned = slotted[...]
    outs[2][...], outs[3][...] = split(turned)
    outs[0][...], outs[1][...] = split(turned.T)


def prepare_kernel(slots, me_ref, heads, tails, pos_head, pos_tail, *rest):
    outs, tail_parts, marks, scratch = rest[:4], rest[4:6], rest[6], rest[7:]
    write_head_parts(me_ref[0], heads[...], outs, *scratch, slots)
    tail_parts[0][...], tail_parts[1][...] = split(tails[...])
    head_rows, tail_rows, pairs = heads.shape[0], tails.shape[0], pos_head.shape[1]
    for bucket in range(2):
        in_head = lax.broadcasted_iota(jnp.int32, (head_rows, pairs), 0) == pos_head[bucket : bucket + 1, :]
        in_tail = lax.broadcasted_iota(jnp.int32, (tail_rows, pairs), 0) == pos_tail[bucket : bucket + 1, :]
        marks[bucket] = lax.dot_general(
            jnp.where(in_head, 1.0, 0.0).astype(BF16),
            jnp.where(in_tail, 1.0, 0.0).astype(BF16),
            NT,
            preferred_element_type=F32,
        )


def bucket_kernel(bucket, slots, *refs):
    blocks, refs = refs[:slots], refs[slots:]
    heads, turned, tails, marks = refs[0:2], refs[2:4], refs[4:6], refs[6]
    relation, product, scores, grad, pieces = refs[7:9], refs[9:11], refs[11], refs[12:14], refs[14:]
    rows = blocks[0].shape[0]
    for r in range(slots):
        at = slice(r * rows, (r + 1) * rows)
        relation[0][at, :], relation[1][at, :] = split(blocks[r][...])
    prod = split(dot3((heads[0][...], heads[1][...]), (relation[0][...], relation[1][...]), NN))
    product[0][...], product[1][...] = prod
    tail = (tails[0][...], tails[1][...])
    grad_scores = (jax.nn.sigmoid(dot3(prod, tail, NT)) - marks[bucket]) * 0.0625
    scores[...] = grad_scores
    grad_product = split(dot3(split(grad_scores), tail, NN))
    grad[0][...], grad[1][...] = grad_product
    whole = dot3((turned[0][...], turned[1][...]), grad_product, NN)
    for r in range(slots):
        pieces[r][...] = whole[r * rows : (r + 1) * rows, :]


def tails_kernel(grad_scores, product_high, product_low, tails, state, tails_out, state_out):
    grad = dot3(split(grad_scores[...].T), (product_high[...], product_low[...]), NN)
    tails_out[...], state_out[...] = adagrad(tails[...], state[...], grad)


def heads_kernel(slots, last, me_ref, grad_high, grad_low, rel_high, rel_low, heads, state, *rest):
    heads_out, state_out, rest = rest[0], rest[1], rest[2:]
    outs, rest = (None, rest) if last else (rest[:4], rest[4:])
    high, low = rest[0], rest[1]
    from_slots(me_ref[0], rel_high, high, slots)
    from_slots(me_ref[0], rel_low, low, slots)
    grad = dot3((grad_high[...], grad_low[...]), (high[...], low[...]), NT)
    new_heads, state_out[...] = adagrad(heads[...], state[...], grad)
    heads_out[...] = new_heads
    if not last:
        write_head_parts(me_ref[0], new_heads, outs, *rest[2:], slots)


def split_kernel(tails, high, low):
    high[...], low[...] = split(tails[...])


def relation_kernel(relation, state, *rest):
    pieces, (relation_out, state_out) = rest[:-2], rest[-2:]
    grad = pieces[0][...]
    for piece in pieces[1:]:
        grad = grad + piece[...]
    relation_out[...], state_out[...] = adagrad(relation[...], state[...], grad)


def call(kernel, outs, args, scratch=(), smem_first=False, flops=0):
    specs = [VMEM] * len(args)
    if smem_first:
        specs[0] = SMEM
    moved = sum(a.size * a.dtype.itemsize for a in args)
    return pl.pallas_call(
        kernel,
        out_shape=[jax.ShapeDtypeStruct(s, t) for s, t in outs],
        in_specs=specs,
        out_specs=[VMEM] * len(outs),
        scratch_shapes=[pltpu.VMEM(s, t) for s, t in scratch],
        compiler_params=pltpu.CompilerParams(vmem_limit_bytes=48 * 1024 * 1024),
        cost_estimate=pl.CostEstimate(flops=flops, bytes_accessed=moved, transcendentals=0),
    )(*args)


def partner(value, mask):
    n = lax.axis_size("blk")
    return lax.ppermute(value, "blk", [(i, i ^ mask) for i in range(n)])


def gather_blocks(own):
    n = lax.axis_size("blk")
    far = range(4, n, 4)
    got = {0: own, 2: partner(own, 2)}
    for k in far:
        got[k] = partner(own, k)
    for k in far:
        got[k ^ 2] = partner(got[k], 2)
    for k in (0, *far):
        got[k ^ 1] = partner(got[k], 1)
        got[k ^ 3] = partner(got[k ^ 2], 1)
    return [got[r] for r in range(n)]


def scatter_blocks(pieces):
    n = len(pieces)
    terms = []
    for k in (*range(n - 4, 0, -4), 0):
        across = pieces[k ^ 2] + partner(pieces[k ^ 3], 1)
        here = pieces[k] + partner(pieces[k ^ 1], 1)
        here = here + partner(across, 2)
        terms.append(partner(here, k) if k else here)
    return terms


def body(heads, head_state, tails, tail_state, relation, relation_state, pos_head, pos_tail):
    share, width = relation.shape
    n = lax.axis_size("blk")
    by_blocks = share % 16 == 0 and n & (n - 1) == 0 and n >= 4
    slots = n if by_blocks else 1
    me = (lax.axis_index("blk").astype(jnp.int32) if by_blocks else jnp.int32(0)).reshape(1)
    head_rows, tail_rows = heads.shape[0], tails.shape[0]
    head_state, tail_state, relation_state = (s.reshape(1, -1) for s in (head_state, tail_state, relation_state))

    def gathered(rows):
        return gather_blocks(rows) if by_blocks else [lax.all_gather(rows, "blk", axis=0, tiled=True)]

    def scattered(pieces):
        if by_blocks:
            return scatter_blocks(pieces)
        return [lax.psum_scatter(pieces[0], "blk", scatter_dimension=0, tiled=True)]

    head_parts = [((head_rows, width), BF16)] * 2 + [((width, head_rows), BF16)] * 2
    turned = [((width, head_rows), F32)] * 2
    tail_parts = [((tail_rows, width), BF16)] * 2
    relation_parts = [((width, width), BF16)] * 2
    row_parts = [((head_rows, width), BF16)] * 2
    block = ((width // slots, width), F32)
    table = ((head_rows, tail_rows), F32)

    *parts, marks = call(
        functools.partial(prepare_kernel, slots),
        [*head_parts, *tail_parts, ((2, *table[0]), F32)],
        [me, heads, tails, pos_head, pos_tail],
        scratch=turned,
        smem_first=True,
    )
    head_half, tail_half = parts[:4], parts[4:]
    for bucket in range(2):
        last = bucket == 1
        blocks = gathered(relation)
        out = call(
            functools.partial(bucket_kernel, bucket, slots),
            [*relation_parts, *row_parts, table, *row_parts, *[block] * slots],
            [*blocks, *head_half, *tail_half, marks],
            flops=6 * head_rows * width * (2 * width + 2 * tail_rows),
        )
        relation_half, product, grad_scores, grad_product, pieces = out[0:2], out[2:4], out[4], out[5:7], out[7:]
        terms = scattered(pieces)
        tails, tail_state = call(
            tails_kernel,
            [(tails.shape, F32), (tail_state.shape, F32)],
            [grad_scores, *product, tails, tail_state],
            flops=6 * head_rows * width * tail_rows,
        )
        if not last:
            tails, tail_state = (
                lax.ppermute(v, "blk", [(i, (i + 1) % n) for i in range(n)]) for v in (tails, tail_state)
            )
            tail_half = call(split_kernel, tail_parts, [tails])
        out = call(
            functools.partial(heads_kernel, slots, last),
            [(heads.shape, F32), (head_state.shape, F32), *([] if last else head_parts)],
            [me, *grad_product, *relation_half, heads, head_state],
            scratch=[*relation_parts, *([] if last else turned)],
            smem_first=True,
            flops=6 * head_rows * width * width,
        )
        heads, head_state, head_half = out[0], out[1], out[2:]
        relation, relation_state = call(
            relation_kernel,
            [(relation.shape, F32), (relation_state.shape, F32)],
            [relation, relation_state, *terms],
        )
    return (
        heads,
        head_state.reshape(-1),
        tails,
        tail_state.reshape(-1),
        relation,
        relation_state.reshape(-1),
    )


def solution(mesh):
    rows, flat, pairs = P(("grp", "blk"), None), P(("grp", "blk")), P(None, ("grp", "blk"))
    return jax.shard_map(
        body,
        mesh=mesh,
        in_specs=(rows, flat, rows, flat, rows, flat, pairs, pairs),
        out_specs=(rows, flat, rows, flat, rows, flat),
        check_vma=False,
    )
```

```python
import functools

import jax
import jax.numpy as jnp
from jax import lax
from jax.experimental import pallas as pl
from jax.experimental.pallas import tpu as pltpu
from jax.sharding import PartitionSpec as P

F32 = jnp.float32
BF16 = jnp.bfloat16
NN = (((1,), (0,)), ((), ()))
NT = (((1,), (1,)), ((), ()))
VMEM = pl.BlockSpec(memory_space=pltpu.VMEM)
SMEM = pl.BlockSpec(memory_space=pltpu.SMEM)


def split(x):
    high = x.astype(BF16)
    return high, (x - high.astype(F32)).astype(BF16)


def dot3(a, b, dims):
    def one(p, q):
        return lax.dot_general(p, q, dims, preferred_element_type=F32)

    return one(a[0], b[0]) + (one(a[0], b[1]) + one(a[1], b[0]))


def diagonal(n):
    return lax.broadcasted_iota(jnp.int32, (n, n), 0) == lax.broadcasted_iota(jnp.int32, (n, n), 1)


def adagrad(param, state_row, grad):
    n = param.shape[0]
    eye = diagonal(n)
    state = jnp.sum(jnp.where(eye, state_row, 0.0), axis=1, keepdims=True)
    state = state + jnp.sum(grad * grad, axis=1, keepdims=True) * (1.0 / grad.shape[1])
    back = jnp.sum(jnp.where(eye, state, 0.0), axis=0, keepdims=True)
    return param - grad * (0.1 / jnp.sqrt(state)), back


def to_slots(me, source, target, slots):
    rows = source.shape[0] // slots
    for r in range(slots):
        start = pl.multiple_of((me ^ r) * rows, rows)
        target[r * rows : (r + 1) * rows, :] = source[pl.ds(start, rows), :]


def from_slots(me, source, target, slots):
    rows = source.shape[0] // slots
    for r in range(slots):
        start = pl.multiple_of((me ^ r) * rows, rows)
        target[pl.ds(start, rows), :] = source[r * rows : (r + 1) * rows, :]


def write_head_parts(me, heads, outs, normal, slotted, slots):
    normal[...] = heads.T
    to_slots(me, normal, slotted, slots)
    turned = slotted[...]
    outs[2][...], outs[3][...] = split(turned)
    outs[0][...], outs[1][...] = split(turned.T)


def prepare_kernel(slots, me_ref, heads, tails, pos_head, pos_tail, *rest):
    outs, tail_parts, marks, scratch = rest[:4], rest[4:6], rest[6], rest[7:]
    write_head_parts(me_ref[0], heads[...], outs, *scratch, slots)
    tail_parts[0][...], tail_parts[1][...] = split(tails[...])
    head_rows, tail_rows, pairs = heads.shape[0], tails.shape[0], pos_head.shape[1]
    for bucket in range(2):
        in_head = lax.broadcasted_iota(jnp.int32, (head_rows, pairs), 0) == pos_head[bucket : bucket + 1, :]
        in_tail = lax.broadcasted_iota(jnp.int32, (tail_rows, pairs), 0) == pos_tail[bucket : bucket + 1, :]
        marks[bucket] = lax.dot_general(
            jnp.where(in_head, 1.0, 0.0).astype(BF16),
            jnp.where(in_tail, 1.0, 0.0).astype(BF16),
            NT,
            preferred_element_type=F32,
        )


def bucket_kernel(bucket, slots, *refs):
    blocks, refs = refs[:slots], refs[slots:]
    heads, turned, tails, marks = refs[0:2], refs[2:4], refs[4:6], refs[6]
    relation, product, scores, grad, pieces = refs[7:9], refs[9:11], refs[11], refs[12:14], refs[14:]
    rows = blocks[0].shape[0]
    for r in range(slots):
        at = slice(r * rows, (r + 1) * rows)
        relation[0][at, :], relation[1][at, :] = split(blocks[r][...])
    prod = split(dot3((heads[0][...], heads[1][...]), (relation[0][...], relation[1][...]), NN))
    product[0][...], product[1][...] = prod
    tail = (tails[0][...], tails[1][...])
    grad_scores = (jax.nn.sigmoid(dot3(prod, tail, NT)) - marks[bucket]) * 0.0625
    scores[...] = grad_scores
    grad_product = split(dot3(split(grad_scores), tail, NN))
    grad[0][...], grad[1][...] = grad_product
    whole = dot3((turned[0][...], turned[1][...]), grad_product, NN)
    for r in range(slots):
        pieces[r][...] = whole[r * rows : (r + 1) * rows, :]


def tails_kernel(grad_scores, product_high, product_low, tails, state, *outs):
    rows = grad_scores.shape[1]
    grad = dot3(split(grad_scores[...].T), (product_high[...], product_low[...]), NN)
    first = state.shape[0] - 1 if state.shape[0] == 1 else rows
    new, new_state = adagrad(tails[:rows, :], state[first : first + 1, :rows], grad)
    if len(outs) == 2:
        outs[0][...], outs[1][...] = new, new_state
    else:
        outs[0][:rows, :] = new
        outs[0][rows:, :] = jnp.zeros((outs[0].shape[0] - rows, outs[0].shape[1]), F32)
        outs[0][rows : rows + 1, :rows] = new_state


def heads_kernel(slots, last, me_ref, grad_high, grad_low, rel_high, rel_low, heads, state, *rest):
    heads_out, state_out, rest = rest[0], rest[1], rest[2:]
    outs, rest = (None, rest) if last else (rest[:4], rest[4:])
    high, low = rest[0], rest[1]
    from_slots(me_ref[0], rel_high, high, slots)
    from_slots(me_ref[0], rel_low, low, slots)
    grad = dot3((grad_high[...], grad_low[...]), (high[...], low[...]), NT)
    new_heads, state_out[...] = adagrad(heads[...], state[...], grad)
    heads_out[...] = new_heads
    if not last:
        write_head_parts(me_ref[0], new_heads, outs, *rest[2:], slots)


def split_kernel(tails, high, low):
    high[...], low[...] = split(tails[: high.shape[0], :])


def relation_kernel(relation, state, *rest):
    pieces, (relation_out, state_out) = rest[:-2], rest[-2:]
    grad = pieces[0][...]
    for piece in pieces[1:]:
        grad = grad + piece[...]
    relation_out[...], state_out[...] = adagrad(relation[...], state[...], grad)


def call(kernel, outs, args, scratch=(), smem_first=False, flops=0):
    specs = [VMEM] * len(args)
    if smem_first:
        specs[0] = SMEM
    moved = sum(a.size * a.dtype.itemsize for a in args)
    return pl.pallas_call(
        kernel,
        out_shape=[jax.ShapeDtypeStruct(s, t) for s, t in outs],
        in_specs=specs,
        out_specs=[VMEM] * len(outs),
        scratch_shapes=[pltpu.VMEM(s, t) for s, t in scratch],
        compiler_params=pltpu.CompilerParams(vmem_limit_bytes=20 * 1024 * 1024),
        cost_estimate=pl.CostEstimate(flops=flops, bytes_accessed=moved, transcendentals=0),
    )(*args)


def partner(value, mask):
    n = lax.axis_size("blk")
    return lax.ppermute(value, "blk", [(i, i ^ mask) for i in range(n)])


def after(value, *others):
    return lax.optimization_barrier((value, *others))[0]


def gather_blocks(own, beside=None):
    n = lax.axis_size("blk")
    far = range(4, n, 4)
    got = {0: own}
    for k in (*far, 2):
        got[k] = partner(own, k)
    if beside:
        got[4] = after(got[4], *beside())
    for k in far:
        got[k ^ 2] = partner(got[k], 2)
    before = ()
    for k in (0, *far):
        first, second = after(got[k], *before), after(got[k ^ 2], *before)
        got[k ^ 1], got[k ^ 3] = partner(first, 1), partner(second, 1)
        before = got[k ^ 1], got[k ^ 3]
    return [got[r] for r in range(n)]


def scatter_blocks(pieces):
    n = len(pieces)
    order = (*range(n - 4, 0, -4), 0)
    across = {k: pieces[k ^ 2] + partner(pieces[k ^ 3], 1) for k in order}
    here = {k: pieces[k] + partner(pieces[k ^ 1], 1) for k in order}
    terms = []
    for k in order:
        total = here[k] + partner(across[k], 2)
        terms.append(partner(total, k) if k else total)
    return terms, [across[k] for k in order]


def body(heads, head_state, tails, tail_state, relation, relation_state, pos_head, pos_tail):
    share, width = relation.shape
    n = lax.axis_size("blk")
    by_blocks = share % 16 == 0 and n & (n - 1) == 0 and n >= 4
    slots = n if by_blocks else 1
    me = (lax.axis_index("blk").astype(jnp.int32) if by_blocks else jnp.int32(0)).reshape(1)
    head_rows, (tail_rows, _), tails_shape = heads.shape[0], tails.shape, tails.shape
    head_state, tail_state, relation_state = (s.reshape(1, -1) for s in (head_state, tail_state, relation_state))

    def gathered(rows, beside=None):
        return gather_blocks(rows, beside) if by_blocks else [lax.all_gather(rows, "blk", axis=0, tiled=True)]

    def scattered(pieces):
        if by_blocks:
            return scatter_blocks(pieces)
        return [lax.psum_scatter(pieces[0], "blk", scatter_dimension=0, tiled=True)], []

    head_parts = [((head_rows, width), BF16)] * 2 + [((width, head_rows), BF16)] * 2
    turned = [((width, head_rows), F32)] * 2
    tail_parts = [((tail_rows, width), BF16)] * 2
    relation_parts = [((width, width), BF16)] * 2
    row_parts = [((head_rows, width), BF16)] * 2
    block = ((width // slots, width), F32)
    table = ((head_rows, tail_rows), F32)

    *parts, marks = call(
        functools.partial(prepare_kernel, slots),
        [*head_parts, *tail_parts, ((2, *table[0]), F32)],
        [me, heads, tails, pos_head, pos_tail],
        scratch=turned,
        smem_first=True,
    )
    head_half, tail_half = parts[:4], parts[4:]
    for bucket in range(2):
        last = bucket == 1
        blocks = gathered(relation, lambda: list(parts) + [marks]) if bucket == 0 else gathered(relation)
        out = call(
            functools.partial(bucket_kernel, bucket, slots),
            [*relation_parts, *row_parts, table, *row_parts, *[block] * slots],
            [*blocks, *head_half, *tail_half, marks],
            flops=6 * head_rows * width * (2 * width + 2 * tail_rows),
        )
        relation_half, product, grad_scores, grad_product, pieces = out[0:2], out[2:4], out[4], out[5:7], out[7:]
        terms, summed = scattered(pieces)
        grown = (tail_rows + 8, width)
        out = call(
            tails_kernel,
            [(tails_shape, F32), (tail_state.shape, F32)] if last else [(grown, F32)],
            [after(grad_scores, *summed), *product, tails, tails if last else tail_state],
            flops=6 * head_rows * width * tail_rows,
        )
        if last:
            tails, tail_state = out
        else:
            tails = lax.ppermute(out[0], "blk", [(i, (i + 1) % n) for i in range(n)])
            tail_half = call(split_kernel, tail_parts, [tails])
        out = call(
            functools.partial(heads_kernel, slots, last),
            [(heads.shape, F32), (head_state.shape, F32), *([] if last else head_parts)],
            [me, after(grad_product[0], *summed), grad_product[1], *relation_half, heads, head_state],
            scratch=[*relation_parts, *([] if last else turned)],
            smem_first=True,
            flops=6 * head_rows * width * width,
        )
        heads, head_state, head_half = out[0], out[1], out[2:]
        relation, relation_state = call(
            relation_kernel,
            [(relation.shape, F32), (relation_state.shape, F32)],
            [relation, relation_state, *terms],
        )
    return (
        heads,
        head_state.reshape(-1),
        tails,
        tail_state.reshape(-1),
        relation,
        relation_state.reshape(-1),
    )


def solution(mesh):
    rows, flat, pairs = P(("grp", "blk"), None), P(("grp", "blk")), P(None, ("grp", "blk"))
    return jax.shard_map(
        body,
        mesh=mesh,
        in_specs=(rows, flat, rows, flat, rows, flat, pairs, pairs),
        out_specs=(rows, flat, rows, flat, rows, flat),
        check_vma=False,
    )
```

```python
import functools

import jax
import jax.numpy as jnp
from jax import lax
from jax.experimental import pallas as pl
from jax.experimental.pallas import tpu as pltpu
from jax.sharding import PartitionSpec as P

F32 = jnp.float32
BF16 = jnp.bfloat16
NN = (((1,), (0,)), ((), ()))
NT = (((1,), (1,)), ((), ()))
VMEM = pl.BlockSpec(memory_space=pltpu.VMEM)
SMEM = pl.BlockSpec(memory_space=pltpu.SMEM)
CHUNKS = 2


def split(x):
    high = x.astype(BF16)
    return high, (x - high.astype(F32)).astype(BF16)


def dot3(a, b, dims):
    def one(p, q):
        return lax.dot_general(p, q, dims, preferred_element_type=F32)

    return one(a[0], b[0]) + (one(a[0], b[1]) + one(a[1], b[0]))


def diagonal(n):
    return lax.broadcasted_iota(jnp.int32, (n, n), 0) == lax.broadcasted_iota(jnp.int32, (n, n), 1)


def adagrad(param, state_row, grad):
    n = param.shape[0]
    eye = diagonal(n)
    state = jnp.sum(jnp.where(eye, state_row, 0.0), axis=1, keepdims=True)
    state = state + jnp.sum(grad * grad, axis=1, keepdims=True) * (1.0 / grad.shape[1])
    back = jnp.sum(jnp.where(eye, state, 0.0), axis=0, keepdims=True)
    return param - grad * (0.1 / jnp.sqrt(state)), back


def to_slots(me, source, target, slots):
    rows = source.shape[0] // slots
    for r in range(slots):
        start = pl.multiple_of((me ^ r) * rows, rows)
        target[r * rows : (r + 1) * rows, :] = source[pl.ds(start, rows), :]


def from_slots(me, source, target, slots, first):
    rows = target.shape[0] // slots
    count = source.shape[0] // rows
    for r in range(count):
        start = pl.multiple_of((me ^ (first + r)) * rows, rows)
        target[pl.ds(start, rows), :] = source[r * rows : (r + 1) * rows, :]
    return first + count


def write_head_parts(me, heads, outs, normal, slotted, slots):
    normal[...] = heads.T
    to_slots(me, normal, slotted, slots)
    outs[0][...], outs[1][...] = split(slotted[...])
    at = 0
    for high, low in zip(outs[2::2], outs[3::2]):
        columns = high.shape[1]
        high[...], low[...] = split(slotted[at : at + columns, :].T)
        at += columns


def prepare_heads_kernel(slots, me_ref, heads, *rest):
    write_head_parts(me_ref[0], heads[...], rest[:-2], *rest[-2:], slots)


def prepare_tails_kernel(head_rows, tails, pos_head, pos_tail, high, low, marks):
    high[...], low[...] = split(tails[...])
    tail_rows, pairs = tails.shape[0], pos_head.shape[1]
    for bucket in range(2):
        in_head = lax.broadcasted_iota(jnp.int32, (head_rows, pairs), 0) == pos_head[bucket : bucket + 1, :]
        in_tail = lax.broadcasted_iota(jnp.int32, (tail_rows, pairs), 0) == pos_tail[bucket : bucket + 1, :]
        marks[bucket] = lax.dot_general(
            jnp.where(in_head, 1.0, 0.0).astype(BF16),
            jnp.where(in_tail, 1.0, 0.0).astype(BF16),
            NT,
            preferred_element_type=F32,
        )


def add_product(blocks, heads, parts):
    rows = blocks[0].shape[0]
    for r, block in enumerate(blocks):
        at = slice(r * rows, (r + 1) * rows)
        parts[0][at, :], parts[1][at, :] = split(block[...])
    return dot3((heads[0][...], heads[1][...]), (parts[0][...], parts[1][...]), NN)


def product_kernel(first, count, *refs):
    before, refs = (None, refs) if first else (refs[0], refs[1:])
    blocks, heads, product, parts = refs[:count], refs[count : count + 2], refs[count + 2], refs[count + 3 :]
    term = add_product(blocks, heads, parts)
    product[...] = term if first else before[...] + term


def bucket_kernel(bucket, first, count, picks, *refs):
    before, refs = (None, refs) if first else (refs[0], refs[1:])
    blocks, refs = refs[:count], refs[count:]
    heads, turned, tails, marks = refs[0:2], refs[2:4], refs[4:6], refs[6]
    relation, product, scores, grad, pieces = refs[7:9], refs[9:11], refs[11], refs[12:14], refs[14:]
    whole = add_product(blocks, heads, relation)
    prod = split(whole if first else before[...] + whole)
    product[0][...], product[1][...] = prod
    tail = (tails[0][...], tails[1][...])
    grad_scores = (jax.nn.sigmoid(dot3(prod, tail, NT)) - marks[bucket]) * 0.0625
    scores[...] = grad_scores
    grad_product = split(dot3(split(grad_scores), tail, NN))
    grad[0][...], grad[1][...] = grad_product
    whole = dot3((turned[0][...], turned[1][...]), grad_product, NN)
    rows = whole.shape[0] // sum(len(slots) for slots in picks)
    for piece, slots in zip(pieces, picks):
        for i, r in enumerate(slots):
            piece[i * rows : (i + 1) * rows, :] = whole[r * rows : (r + 1) * rows, :]


def tails_kernel(chunks, last, grad_scores, product_high, product_low, *refs):
    grad = dot3(split(grad_scores[...].T), (product_high[...], product_low[...]), NN)
    if last:
        tails, outs = refs[:chunks], refs[chunks:]
        rows = [outs[0].shape[0] // chunks] * chunks
        state = tails[-1][rows[-1] : rows[-1] + 1, : outs[0].shape[0]]
        held = [t[:n, :] for t, n in zip(tails, rows)]
        outs[0][...], outs[1][...] = adagrad(jnp.concatenate(held, axis=0), state, grad)
        return
    tails, state, outs = refs[0], refs[1], refs[2:]
    new, new_state = adagrad(tails[...], state[...], grad)
    rows = tails.shape[0] // chunks
    for c in range(chunks):
        outs[c][:rows, :] = new[c * rows : (c + 1) * rows, :]
    outs[-1][rows:, :] = jnp.zeros((outs[-1].shape[0] - rows, new.shape[1]), F32)
    outs[-1][rows : rows + 1, : tails.shape[0]] = new_state


def heads_kernel(slots, groups, last, me_ref, grad_high, grad_low, *rest):
    relation, (heads, state, heads_out, state_out), rest = rest[: 2 * groups], rest[2 * groups : 2 * groups + 4], rest[2 * groups + 4 :]
    outs, (high, low) = rest[: 2 + 2 * groups], (rest[:2] if last else rest[2 + 2 * groups : 4 + 2 * groups])
    at = 0
    for g in range(groups):
        from_slots(me_ref[0], relation[2 * g], high, slots, at)
        at = from_slots(me_ref[0], relation[2 * g + 1], low, slots, at)
    grad = dot3((grad_high[...], grad_low[...]), (high[...], low[...]), NT)
    new_heads, state_out[...] = adagrad(heads[...], state[...], grad)
    heads_out[...] = new_heads
    if not last:
        write_head_parts(me_ref[0], new_heads, outs, *rest[-2:], slots)


def split_kernel(*refs):
    chunks, (high, low) = refs[:-2], refs[-2:]
    rows = high.shape[0] // len(chunks)
    for c, chunk in enumerate(chunks):
        at = slice(c * rows, (c + 1) * rows)
        high[at, :], low[at, :] = split(chunk[:rows, :])


def sum_kernel(a, b, *totals):
    at = 0
    for total in totals:
        rows = slice(at, at + total.shape[0])
        total[...] = a[rows, :] + b[rows, :]
        at += total.shape[0]


def total_kernel(place, a, b, c, total):
    rows = slice(place * total.shape[0], (place + 1) * total.shape[0])
    total[...] = a[rows, :] + b[rows, :] + c[...]


def relation_kernel(relation, state, *rest):
    pieces, (relation_out, state_out) = rest[:-2], rest[-2:]
    grad = pieces[0][...]
    for piece in pieces[1:]:
        grad = grad + piece[...]
    relation_out[...], state_out[...] = adagrad(relation[...], state[...], grad)


def call(kernel, outs, args, scratch=(), smem_first=False, flops=0):
    specs = [VMEM] * len(args)
    if smem_first:
        specs[0] = SMEM
    moved = sum(a.size * a.dtype.itemsize for a in args)
    return pl.pallas_call(
        kernel,
        out_shape=[jax.ShapeDtypeStruct(s, t) for s, t in outs],
        in_specs=specs,
        out_specs=[VMEM] * len(outs),
        scratch_shapes=[pltpu.VMEM(s, t) for s, t in scratch],
        compiler_params=pltpu.CompilerParams(vmem_limit_bytes=20 * 1024 * 1024),
        cost_estimate=pl.CostEstimate(flops=flops, bytes_accessed=moved, transcendentals=0),
    )(*args)


def partner(value, mask):
    n = lax.axis_size("blk")
    return lax.ppermute(value, "blk", [(i, i ^ mask) for i in range(n)])


def after(value, *others):
    return lax.optimization_barrier((value, *others))[0]


def gather_groups(own, early, late, crowded, use):
    n = lax.axis_size("blk")
    far = list(range(4, n, 4))
    got = {0: own}
    step = n // 2
    while step >= 4:
        for k in [k for k in (0, *far) if k in got]:
            got[k ^ step] = partner(got[k], step)
        if step == n // 2:
            got[step] = after(got[step], *early)
        step //= 2
    for k in (0, *far):
        ready = after(got[k], got[k]) if crowded and k != far[-1] else got[k]
        got[k ^ 2] = partner(ready, 2)
    waited = late
    for k in (0, *far):
        first = after(got[k], *waited) if k == far[-1] else got[k]
        got[k ^ 1], got[k ^ 3] = partner(first, 1), partner(got[k ^ 2], 1)
        out = use([got[k ^ r] for r in range(4)], k == far[-1])
        if k == 0:
            waited = [*waited, out]
    return out


def pick_slots(n):
    order = (*range(n - 4, 0, -4), 0)
    return [[k ^ r for k in order] for r in (2, 3, 0, 1)]


def scatter_blocks(n, across, across_far, here, here_far):
    order = (*range(n - 4, 0, -4), 0)
    share = across.shape[0] // len(order)
    shape = ((share, across.shape[1]), F32)
    turned = partner(across_far, 1), partner(here_far, 1)
    sent = call(sum_kernel, [shape] * len(order), [across, turned[0]])
    crossed = [partner(value, 2) for value in sent]
    totals = {
        k: call(functools.partial(total_kernel, i), [shape], [here, turned[1], crossed[i]])[0]
        for i, k in enumerate(order)
    }
    step = 4
    while step < n // 2:
        for k in [k for k in totals if k & step]:
            (totals[k ^ step],) = call(sum_kernel, [shape], [totals[k ^ step], partner(totals.pop(k), step)])
        step *= 2
    return [totals[0], partner(totals[step], step)], crossed


def body(heads, head_state, tails, tail_state, relation, relation_state, pos_head, pos_tail):
    share, width = relation.shape
    n = lax.axis_size("blk")
    by_blocks = share % 16 == 0 and n & (n - 1) == 0 and n >= 16
    slots = n if by_blocks else 1
    me = (lax.axis_index("blk").astype(jnp.int32) if by_blocks else jnp.int32(0)).reshape(1)
    head_rows, tail_rows = heads.shape[0], tails.shape[0]
    head_state, tail_state, relation_state = (s.reshape(1, -1) for s in (head_state, tail_state, relation_state))

    def gathered(rows, early, late, crowded, use):
        if by_blocks:
            return gather_groups(rows, early, late, crowded, use)
        return use([lax.all_gather(rows, "blk", axis=0, tiled=True)], True)

    def scattered(pieces):
        if by_blocks:
            return scatter_blocks(n, *pieces)
        return [lax.psum_scatter(pieces[0], "blk", scatter_dimension=0, tiled=True)], []

    picks = pick_slots(n) if by_blocks else [[0]]
    sizes = [4 * share] * (n // 4) if by_blocks else [width]
    head_parts = [((width, head_rows), BF16)] * 2
    for size in sizes:
        head_parts += [((head_rows, size), BF16)] * 2
    turned = [((width, head_rows), F32)] * 2
    tail_parts = [((tail_rows, width), BF16)] * 2
    relation_parts = [[((size, width), BF16)] * 2 for size in sizes]
    row_parts = [((head_rows, width), BF16)] * 2
    held = [((len(pick) * (width // slots), width), F32) for pick in picks]
    table = ((head_rows, tail_rows), F32)

    head_half = call(
        functools.partial(prepare_heads_kernel, slots), head_parts, [me, heads], scratch=turned, smem_first=True
    )
    *tail_half, marks = call(
        functools.partial(prepare_tails_kernel, head_rows),
        [*tail_parts, ((2, *table[0]), F32)],
        [tails, pos_head, pos_tail],
    )
    for bucket in range(2):
        last = bucket == 1
        before, relation_half = [], []

        def use(blocks, closing):
            first, g = not before, len(relation_half) // 2
            halves, count = head_half[2 + 2 * g : 4 + 2 * g], len(blocks)
            if closing:
                out = call(
                    functools.partial(bucket_kernel, bucket, first, count, picks),
                    [*relation_parts[g], *row_parts, table, *row_parts, *held],
                    [*before[-1:], *blocks, *halves, *head_half[:2], *tail_half, marks],
                    flops=6 * head_rows * width * (2 * width + 2 * tail_rows),
                )
                relation_half.extend(out[:2])
                return out
            out = call(
                functools.partial(product_kernel, first, count),
                [((head_rows, width), F32), *relation_parts[g]],
                [*before[-1:], *blocks, *halves],
                flops=100000000,
            )
            relation_half.extend(out[1:])
            before.append(out[0])
            return out[0]

        out = gathered(relation, head_half, [] if bucket else [*tail_half, marks], bucket == 1, use)
        product, grad_scores, grad_product, pieces = out[2:4], out[4], out[5:7], out[7:]
        terms, crossed = scattered(pieces)
        tail_rest = {"flops": 6 * head_rows * width * tail_rows}
        if not last:
            rows = tail_rows // CHUNKS
            sent = call(
                functools.partial(tails_kernel, CHUNKS, last),
                [((rows, width), F32)] * (CHUNKS - 1) + [((rows + 8, width), F32)],
                [grad_scores, *product, tails, tail_state],
                **tail_rest,
            )
            sent = [after(v, *()) for v in sent]
            tails = [lax.ppermute(v, "blk", [(i, (i + 1) % n) for i in range(n)]) for v in sent]
            tail_half = call(split_kernel, tail_parts, tails)
        else:
            tails, tail_state = call(
                functools.partial(tails_kernel, CHUNKS, last),
                [((tail_rows, width), F32), (tail_state.shape, F32)],
                [after(grad_scores, *crossed[-1:]), *product, *tails],
                **tail_rest,
            )
        out = call(
            functools.partial(heads_kernel, slots, len(sizes), last),
            [(heads.shape, F32), (head_state.shape, F32), *([] if last else head_parts)],
            [me, after(grad_product[0], *crossed[-1:]), grad_product[1], *relation_half, heads, head_state],
            scratch=[((width, width), BF16)] * 2 + ([] if last else turned),
            smem_first=True,
        )
        heads, head_state, head_half = out[0], out[1], out[2:]
        relation, relation_state = call(
            relation_kernel,
            [(relation.shape, F32), (relation_state.shape, F32)],
            [relation, relation_state, *terms],
        )
    return (
        heads,
        head_state.reshape(-1),
        tails,
        tail_state.reshape(-1),
        relation,
        relation_state.reshape(-1),
    )


def solution(mesh):
    rows, flat, pairs = P(("grp", "blk"), None), P(("grp", "blk")), P(None, ("grp", "blk"))
    return jax.shard_map(
        body,
        mesh=mesh,
        in_specs=(rows, flat, rows, flat, rows, flat, pairs, pairs),
        out_specs=(rows, flat, rows, flat, rows, flat),
        check_vma=False,
    )
```

```python
import functools

import jax
import jax.numpy as jnp
from jax import lax
from jax.experimental import pallas as pl
from jax.experimental.pallas import tpu as pltpu
from jax.sharding import PartitionSpec as P

F32 = jnp.float32
BF16 = jnp.bfloat16
NN = (((1,), (0,)), ((), ()))
NT = (((1,), (1,)), ((), ()))
VMEM = pl.BlockSpec(memory_space=pltpu.VMEM)
SMEM = pl.BlockSpec(memory_space=pltpu.SMEM)
CHUNKS = 1


def split(x):
    high = x.astype(BF16)
    return high, (x - high.astype(F32)).astype(BF16)


def dot3(a, b, dims):
    def one(p, q):
        return lax.dot_general(p, q, dims, preferred_element_type=F32)

    return one(a[0], b[0]) + (one(a[0], b[1]) + one(a[1], b[0]))


def diagonal(n):
    return lax.broadcasted_iota(jnp.int32, (n, n), 0) == lax.broadcasted_iota(jnp.int32, (n, n), 1)


def adagrad(param, state_row, grad):
    n = param.shape[0]
    eye = diagonal(n)
    state = jnp.sum(jnp.where(eye, state_row, 0.0), axis=1, keepdims=True)
    state = state + jnp.sum(grad * grad, axis=1, keepdims=True) * (1.0 / grad.shape[1])
    back = jnp.sum(jnp.where(eye, state, 0.0), axis=0, keepdims=True)
    return param - grad * (0.1 / jnp.sqrt(state)), back


def to_slots(me, source, target, slots):
    rows = source.shape[0] // slots
    for r in range(slots):
        start = pl.multiple_of((me ^ r) * rows, rows)
        target[r * rows : (r + 1) * rows, :] = source[pl.ds(start, rows), :]


def from_slots(me, source, target, slots, first):
    rows = target.shape[0] // slots
    count = source.shape[0] // rows
    for r in range(count):
        start = pl.multiple_of((me ^ (first + r)) * rows, rows)
        target[pl.ds(start, rows), :] = source[r * rows : (r + 1) * rows, :]
    return first + count


def write_head_parts(me, heads, outs, normal, slotted, slots):
    normal[...] = heads.T
    to_slots(me, normal, slotted, slots)
    outs[0][...], outs[1][...] = split(slotted[...])
    at = 0
    for high, low in zip(outs[2::2], outs[3::2]):
        columns = high.shape[1]
        high[...], low[...] = split(slotted[at : at + columns, :].T)
        at += columns


def prepare_heads_kernel(slots, me_ref, heads, *rest):
    write_head_parts(me_ref[0], heads[...], rest[:-2], *rest[-2:], slots)


def prepare_tails_kernel(head_rows, tails, pos_head, pos_tail, high, low, marks):
    high[...], low[...] = split(tails[...])
    tail_rows, pairs = tails.shape[0], pos_head.shape[1]
    for bucket in range(2):
        in_head = lax.broadcasted_iota(jnp.int32, (head_rows, pairs), 0) == pos_head[bucket : bucket + 1, :]
        in_tail = lax.broadcasted_iota(jnp.int32, (tail_rows, pairs), 0) == pos_tail[bucket : bucket + 1, :]
        marks[bucket] = lax.dot_general(
            jnp.where(in_head, 1.0, 0.0).astype(BF16),
            jnp.where(in_tail, 1.0, 0.0).astype(BF16),
            NT,
            preferred_element_type=F32,
        )


def add_product(blocks, heads, parts):
    rows = blocks[0].shape[0]
    for r, block in enumerate(blocks):
        at = slice(r * rows, (r + 1) * rows)
        parts[0][at, :], parts[1][at, :] = split(block[...])
    return dot3((heads[0][...], heads[1][...]), (parts[0][...], parts[1][...]), NN)


def product_kernel(first, count, *refs):
    before, refs = (None, refs) if first else (refs[0], refs[1:])
    blocks, heads, product, parts = refs[:count], refs[count : count + 2], refs[count + 2], refs[count + 3 :]
    term = add_product(blocks, heads, parts)
    product[...] = term if first else before[...] + term


def scores_kernel(bucket, first, count, rows, *refs):
    before, refs = (None, refs) if first else (refs[0], refs[1:])
    blocks, refs = refs[:count], refs[count:]
    heads, halves, marks, refs = refs[0:2], refs[2:4], refs[4], refs[5:]
    if rows:
        tails, state, refs = refs[0], refs[1], refs[2:]
    relation, product, scores, chunks = refs[0:2], refs[2:4], refs[4], refs[5:]
    whole = add_product(blocks, heads, relation)
    prod = split(whole if first else before[...] + whole)
    product[0][...], product[1][...] = prod
    grad_scores = (jax.nn.sigmoid(dot3(prod, (halves[0][...], halves[1][...]), NT)) - marks[bucket]) * 0.0625
    scores[...] = grad_scores
    if rows:
        grad = dot3(split(grad_scores.T), prod, NN)
        new, new_state = adagrad(tails[...], state[...], grad)
        at = 0
        for chunk, n in zip(chunks, rows):
            chunk[:n, :] = new[at : at + n, :]
            at += n
        chunks[-1][rows[-1] :, :] = jnp.zeros((chunks[-1].shape[0] - rows[-1], new.shape[1]), F32)
        chunks[-1][rows[-1] : rows[-1] + 1, : tails.shape[0]] = new_state


def grads_kernel(picks, turned_high, turned_low, scores, high, low, *refs):
    grad = split(dot3(split(scores[...]), (high[...], low[...]), NN))
    refs[0][...], refs[1][...] = grad
    relation_term_kernel(picks, turned_high, turned_low, *refs)


def relation_term_kernel(picks, turned_high, turned_low, grad_high, grad_low, *pieces):
    rows = turned_high.shape[0] // picks[0]
    grad = grad_high[...], grad_low[...]
    for piece, slots in zip(pieces, picks[1:]):
        high = jnp.concatenate([turned_high[r * rows : (r + 1) * rows, :] for r in slots], axis=0)
        low = jnp.concatenate([turned_low[r * rows : (r + 1) * rows, :] for r in slots], axis=0)
        piece[...] = dot3((high, low), grad, NN)


def tails_kernel(rows, grad_scores, product_high, product_low, *refs):
    grad = dot3(split(grad_scores[...].T), (product_high[...], product_low[...]), NN)
    tails, outs = refs[: len(rows)], refs[len(rows) :]
    state = tails[-1][rows[-1] : rows[-1] + 1, : outs[0].shape[0]]
    held = [t[:n, :] for t, n in zip(tails, rows)]
    outs[0][...], outs[1][...] = adagrad(jnp.concatenate(held, axis=0), state, grad)


def heads_kernel(slots, groups, last, me_ref, grad_high, grad_low, *rest):
    relation, (heads, state, heads_out, state_out), rest = rest[: 2 * groups], rest[2 * groups : 2 * groups + 4], rest[2 * groups + 4 :]
    outs, (high, low) = rest[: 2 + 2 * groups], (rest[:2] if last else rest[2 + 2 * groups : 4 + 2 * groups])
    at = 0
    for g in range(groups):
        from_slots(me_ref[0], relation[2 * g], high, slots, at)
        at = from_slots(me_ref[0], relation[2 * g + 1], low, slots, at)
    grad = dot3((grad_high[...], grad_low[...]), (high[...], low[...]), NT)
    new_heads, state_out[...] = adagrad(heads[...], state[...], grad)
    heads_out[...] = new_heads
    if not last:
        write_head_parts(me_ref[0], new_heads, outs, *rest[-2:], slots)


def split_kernel(rows, *refs):
    chunks, (high, low) = refs[:-2], refs[-2:]
    at = 0
    for chunk, n in zip(chunks, rows):
        high[at : at + n, :], low[at : at + n, :] = split(chunk[:n, :])
        at += n


def sum_kernel(a, b, *totals):
    at = 0
    for total in totals:
        rows = slice(at, at + total.shape[0])
        total[...] = a[rows, :] + b[rows, :]
        at += total.shape[0]


def total_kernel(place, a, b, c, total):
    rows = slice(place * total.shape[0], (place + 1) * total.shape[0])
    total[...] = a[rows, :] + b[rows, :] + c[...]


def relation_kernel(relation, state, *rest):
    pieces, (relation_out, state_out) = rest[:-2], rest[-2:]
    grad = pieces[0][...]
    for piece in pieces[1:]:
        grad = grad + piece[...]
    relation_out[...], state_out[...] = adagrad(relation[...], state[...], grad)


def call(kernel, outs, args, scratch=(), smem_first=False, flops=0):
    specs = [VMEM] * len(args)
    if smem_first:
        specs[0] = SMEM
    moved = sum(a.size * a.dtype.itemsize for a in args)
    return pl.pallas_call(
        kernel,
        out_shape=[jax.ShapeDtypeStruct(s, t) for s, t in outs],
        in_specs=specs,
        out_specs=[VMEM] * len(outs),
        scratch_shapes=[pltpu.VMEM(s, t) for s, t in scratch],
        compiler_params=pltpu.CompilerParams(vmem_limit_bytes=20 * 1024 * 1024),
        cost_estimate=pl.CostEstimate(flops=flops, bytes_accessed=moved, transcendentals=0),
    )(*args)


def partner(value, mask):
    n = lax.axis_size("blk")
    return lax.ppermute(value, "blk", [(i, i ^ mask) for i in range(n)])


def after(value, *others):
    return lax.optimization_barrier((value, *others))[0]


def gather_groups(own, early, late, crowded, use):
    n = lax.axis_size("blk")
    far = list(range(4, n, 4))
    got = {0: own}
    step = n // 2
    while step >= 4:
        for k in [k for k in (0, *far) if k in got]:
            got[k ^ step] = partner(got[k], step)
        if step == n // 2:
            got[step] = after(got[step], *early)
        step //= 2
    for k in (0, *far):
        ready = after(got[k], got[k]) if crowded and k != far[-1] else got[k]
        got[k ^ 2] = partner(ready, 2)
    waited = late
    for k in (0, *far):
        first = after(got[k], *waited) if k == far[-1] else got[k]
        got[k ^ 1], got[k ^ 3] = partner(first, 1), partner(got[k ^ 2], 1)
        out = use([got[k ^ r] for r in range(4)], k == far[-1])
        if k == 0:
            waited = [*waited, out]
    return out


def pick_slots(n):
    order = (*range(n - 4, 0, -4), 0)
    return [[k ^ r for k in order] for r in (2, 3, 0, 1)]


def scatter_blocks(n, across, across_far, here, here_far):
    order = (*range(n - 4, 0, -4), 0)
    share = across.shape[0] // len(order)
    shape = ((share, across.shape[1]), F32)
    turned = partner(across_far, 1), partner(here_far, 1)
    sent = call(sum_kernel, [shape] * len(order), [across, turned[0]])
    crossed = [partner(value, 2) for value in sent]
    totals = {
        k: call(functools.partial(total_kernel, i), [shape], [here, turned[1], crossed[i]])[0]
        for i, k in enumerate(order)
    }
    step = 4
    while step < n // 2:
        for k in [k for k in totals if k & step]:
            (totals[k ^ step],) = call(sum_kernel, [shape], [totals[k ^ step], partner(totals.pop(k), step)])
        step *= 2
    return [totals[0], partner(totals[step], step)], crossed


def body(heads, head_state, tails, tail_state, relation, relation_state, pos_head, pos_tail):
    share, width = relation.shape
    n = lax.axis_size("blk")
    by_blocks = share % 16 == 0 and n & (n - 1) == 0 and n >= 16
    slots = n if by_blocks else 1
    me = (lax.axis_index("blk").astype(jnp.int32) if by_blocks else jnp.int32(0)).reshape(1)
    head_rows, tail_rows = heads.shape[0], tails.shape[0]
    head_state, tail_state, relation_state = (s.reshape(1, -1) for s in (head_state, tail_state, relation_state))

    def gathered(rows, early, late, crowded, use):
        if by_blocks:
            return gather_groups(rows, early, late, crowded, use)
        return use([lax.all_gather(rows, "blk", axis=0, tiled=True)], True)

    def scattered(pieces):
        if by_blocks:
            return scatter_blocks(n, *pieces)
        return [lax.psum_scatter(pieces[0], "blk", scatter_dimension=0, tiled=True)], []

    picks = pick_slots(n) if by_blocks else [[0]]
    sizes = [4 * share] * (n // 4) if by_blocks else [width]
    head_parts = [((width, head_rows), BF16)] * 2
    for size in sizes:
        head_parts += [((head_rows, size), BF16)] * 2
    turned = [((width, head_rows), F32)] * 2
    tail_parts = [((tail_rows, width), BF16)] * 2
    relation_parts = [[((size, width), BF16)] * 2 for size in sizes]
    row_parts = [((head_rows, width), BF16)] * 2
    held = [((len(pick) * (width // slots), width), F32) for pick in picks]
    table = ((head_rows, tail_rows), F32)

    head_half = call(
        functools.partial(prepare_heads_kernel, slots), head_parts, [me, heads], scratch=turned, smem_first=True
    )
    *tail_half, marks = call(
        functools.partial(prepare_tails_kernel, head_rows),
        [*tail_parts, ((2, *table[0]), F32)],
        [tails, pos_head, pos_tail],
    )
    rows = [tail_rows // CHUNKS] * CHUNKS
    sent_shapes = [((r + 8 * (i == CHUNKS - 1), width), F32) for i, r in enumerate(rows)]
    for bucket in range(2):
        last = bucket == 1
        before, relation_half = [], []

        def use(blocks, closing):
            first, g = not before, len(relation_half) // 2
            halves, count = head_half[2 + 2 * g : 4 + 2 * g], len(blocks)
            if closing:
                out = call(
                    functools.partial(scores_kernel, bucket, first, count, [] if last else rows),
                    [*relation_parts[g], *row_parts, table, *([] if last else sent_shapes)],
                    [*before[-1:], *blocks, *halves, *tail_half, marks, *([] if last else [tails, tail_state])],
                    flops=6 * head_rows * width * (width // len(sizes) + 2 * tail_rows),
                )
                relation_half.extend(out[:2])
                return out
            out = call(
                functools.partial(product_kernel, first, count),
                [((head_rows, width), F32), *relation_parts[g]],
                [*before[-1:], *blocks, *halves],
                flops=100000000,
            )
            relation_half.extend(out[1:])
            before.append(out[0])
            return out[0]

        out = gathered(relation, head_half, [] if bucket else [*tail_half, marks], bucket == 1, use)
        product, grad_scores, sent = out[2:4], out[4], out[5:]
        if not last:
            moves = [(i, (i + 1) % n) for i in range(n)]
            arrived = [lax.ppermute(v, "blk", moves) for v in sent]
        pieces = {}
        for chosen in ((1, 3), (0, 2)) if by_blocks else [(0,)]:
            wanted = [slots, *[picks[c] for c in chosen]]
            shapes = [held[c] for c in chosen]
            if pieces:
                out = call(
                    functools.partial(relation_term_kernel, wanted), shapes, [*head_half[:2], *grad_product], flops=6 * head_rows * width * width // 2
                )
            else:
                out = call(
                    functools.partial(grads_kernel, wanted),
                    [*row_parts, *shapes],
                    [*head_half[:2], grad_scores, *tail_half],
                    flops=6 * head_rows * width * width // 2,
                )
                grad_product, out = out[:2], out[2:]
            pieces.update(zip(chosen, out))
        pieces = [pieces[c] for c in range(len(picks))]
        terms, crossed = scattered(pieces)
        if last:
            tails, tail_state = call(
                functools.partial(tails_kernel, rows),
                [((tail_rows, width), F32), (tail_state.shape, F32)],
                [after(grad_scores, *crossed[-1:]), *product, *tails],
                flops=6 * head_rows * width * tail_rows,
            )
        else:
            tails = arrived
            tail_half = call(functools.partial(split_kernel, rows), tail_parts, tails)
        out = call(
            functools.partial(heads_kernel, slots, len(sizes), last),
            [(heads.shape, F32), (head_state.shape, F32), *([] if last else head_parts)],
            [me, after(grad_product[0], *(crossed[-1:] if last else arrived)), grad_product[1], *relation_half, heads, head_state],
            scratch=[((width, width), BF16)] * 2 + ([] if last else turned),
            smem_first=True,
        )
        heads, head_state, head_half = out[0], out[1], out[2:]
        relation, relation_state = call(
            relation_kernel,
            [(relation.shape, F32), (relation_state.shape, F32)],
            [relation, relation_state, *terms],
        )
    return (
        heads,
        head_state.reshape(-1),
        tails,
        tail_state.reshape(-1),
        relation,
        relation_state.reshape(-1),
    )


def solution(mesh):
    rows, flat, pairs = P(("grp", "blk"), None), P(("grp", "blk")), P(None, ("grp", "blk"))
    return jax.shard_map(
        body,
        mesh=mesh,
        in_specs=(rows, flat, rows, flat, rows, flat, pairs, pairs),
        out_specs=(rows, flat, rows, flat, rows, flat),
        check_vma=False,
    )
```

```python
import functools

import jax
import jax.numpy as jnp
from jax import lax
from jax.experimental import pallas as pl
from jax.experimental.pallas import tpu as pltpu
from jax.sharding import PartitionSpec as P

F32 = jnp.float32
BF16 = jnp.bfloat16
NN = (((1,), (0,)), ((), ()))
NT = (((1,), (1,)), ((), ()))
VMEM = pl.BlockSpec(memory_space=pltpu.VMEM)
SMEM = pl.BlockSpec(memory_space=pltpu.SMEM)
CHUNKS = 1


def split(x):
    high = x.astype(BF16)
    return high, (x - high.astype(F32)).astype(BF16)


def dot3(a, b, dims):
    (((i,), (j,)), _) = dims
    left = jnp.concatenate([a[1], a[0], a[0]], axis=i)
    right = jnp.concatenate([b[0], b[1], b[0]], axis=j)
    return lax.dot_general(left, right, dims, preferred_element_type=F32)


def diagonal(n):
    return lax.broadcasted_iota(jnp.int32, (n, n), 0) == lax.broadcasted_iota(jnp.int32, (n, n), 1)


def adagrad(param, state_row, grad):
    n = param.shape[0]
    eye = diagonal(n)
    state = jnp.sum(jnp.where(eye, state_row, 0.0), axis=1, keepdims=True)
    state = state + jnp.sum(grad * grad, axis=1, keepdims=True) * (1.0 / grad.shape[1])
    back = jnp.sum(jnp.where(eye, state, 0.0), axis=0, keepdims=True)
    return param - grad * (0.1 / jnp.sqrt(state)), back


def to_slots(me, source, target, slots):
    rows = source.shape[0] // slots
    for r in range(slots):
        start = pl.multiple_of((me ^ r) * rows, rows)
        target[r * rows : (r + 1) * rows, :] = source[pl.ds(start, rows), :]


def from_slots(me, source, target, slots, first):
    rows = target.shape[0] // slots
    count = source.shape[0] // rows
    for r in range(count):
        start = pl.multiple_of((me ^ (first + r)) * rows, rows)
        target[pl.ds(start, rows), :] = source[r * rows : (r + 1) * rows, :]
    return first + count


def write_head_parts(me, heads, outs, normal, slotted, slots):
    normal[...] = heads.T
    to_slots(me, normal, slotted, slots)
    outs[0][...], outs[1][...] = split(slotted[...])
    at = 0
    for high, low in zip(outs[2::2], outs[3::2]):
        columns = high.shape[1]
        high[...], low[...] = split(slotted[at : at + columns, :].T)
        at += columns


def prepare_heads_kernel(slots, me_ref, heads, *rest):
    write_head_parts(me_ref[0], heads[...], rest[:-2], *rest[-2:], slots)


def prepare_tails_kernel(head_rows, tails, pos_head, pos_tail, high, low, marks):
    high[...], low[...] = split(tails[...])
    tail_rows, pairs = tails.shape[0], pos_head.shape[1]
    for bucket in range(2):
        in_head = lax.broadcasted_iota(jnp.int32, (head_rows, pairs), 0) == pos_head[bucket : bucket + 1, :]
        in_tail = lax.broadcasted_iota(jnp.int32, (tail_rows, pairs), 0) == pos_tail[bucket : bucket + 1, :]
        marks[bucket] = lax.dot_general(
            jnp.where(in_head, 1.0, 0.0).astype(BF16),
            jnp.where(in_tail, 1.0, 0.0).astype(BF16),
            NT,
            preferred_element_type=F32,
        )


def add_product(blocks, heads, parts):
    rows = blocks[0].shape[0]
    for r, block in enumerate(blocks):
        at = slice(r * rows, (r + 1) * rows)
        parts[0][at, :], parts[1][at, :] = split(block[...])
    return dot3((heads[0][...], heads[1][...]), (parts[0][...], parts[1][...]), NN)


def product_kernel(first, count, *refs):
    before, refs = (None, refs) if first else (refs[0], refs[1:])
    blocks, heads, product, parts = refs[:count], refs[count : count + 2], refs[count + 2], refs[count + 3 :]
    term = add_product(blocks, heads, parts)
    product[...] = term if first else before[...] + term


def scores_kernel(bucket, first, count, rows, *refs):
    before, refs = (None, refs) if first else (refs[0], refs[1:])
    blocks, refs = refs[:count], refs[count:]
    heads, halves, marks, refs = refs[0:2], refs[2:4], refs[4], refs[5:]
    if rows:
        tails, state, refs = refs[0], refs[1], refs[2:]
    relation, product, scores, chunks = refs[0:2], refs[2:4], refs[4], refs[5:]
    whole = add_product(blocks, heads, relation)
    prod = split(whole if first else before[...] + whole)
    product[0][...], product[1][...] = prod
    grad_scores = (jax.nn.sigmoid(dot3(prod, (halves[0][...], halves[1][...]), NT)) - marks[bucket]) * 0.0625
    scores[...] = grad_scores
    if rows:
        grad = dot3(split(grad_scores.T), prod, NN)
        new, new_state = adagrad(tails[...], state[...], grad)
        at = 0
        for chunk, n in zip(chunks, rows):
            chunk[:n, :] = new[at : at + n, :]
            at += n
        chunks[-1][rows[-1] :, :] = jnp.zeros((chunks[-1].shape[0] - rows[-1], new.shape[1]), F32)
        chunks[-1][rows[-1] : rows[-1] + 1, : tails.shape[0]] = new_state


def grads_kernel(picks, turned_high, turned_low, scores, high, low, *refs):
    grad = split(dot3(split(scores[...]), (high[...], low[...]), NN))
    refs[0][...], refs[1][...] = grad
    relation_term_kernel(picks, turned_high, turned_low, *refs)


def relation_term_kernel(picks, turned_high, turned_low, grad_high, grad_low, *pieces):
    rows = turned_high.shape[0] // picks[0]
    grad = grad_high[...], grad_low[...]
    for piece, slots in zip(pieces, picks[1:]):
        high = jnp.concatenate([turned_high[r * rows : (r + 1) * rows, :] for r in slots], axis=0)
        low = jnp.concatenate([turned_low[r * rows : (r + 1) * rows, :] for r in slots], axis=0)
        piece[...] = dot3((high, low), grad, NN)


def scores_and_grads_kernel(bucket, first, count, picks, *refs):
    held = count + (not first)
    inputs, (turned_high, turned_low), outs = refs[: held + 5], refs[held + 5 : held + 7], refs[held + 7 :]
    scores_kernel(bucket, first, count, [], *inputs, *outs[:5])
    grads_kernel(picks, turned_high, turned_low, outs[4], *inputs[held + 2 : held + 4], *outs[5:])


def tails_kernel(rows, grad_scores, product_high, product_low, *refs):
    grad = dot3(split(grad_scores[...].T), (product_high[...], product_low[...]), NN)
    tails, outs = refs[: len(rows)], refs[len(rows) :]
    state = tails[-1][rows[-1] : rows[-1] + 1, : outs[0].shape[0]]
    held = [t[:n, :] for t, n in zip(tails, rows)]
    outs[0][...], outs[1][...] = adagrad(jnp.concatenate(held, axis=0), state, grad)


def heads_kernel(slots, groups, last, me_ref, grad_high, grad_low, *rest):
    relation, (heads, state, heads_out, state_out), rest = rest[: 2 * groups], rest[2 * groups : 2 * groups + 4], rest[2 * groups + 4 :]
    outs, (high, low) = rest[: 2 + 2 * groups], (rest[:2] if last else rest[2 + 2 * groups : 4 + 2 * groups])
    at = 0
    for g in range(groups):
        from_slots(me_ref[0], relation[2 * g], high, slots, at)
        at = from_slots(me_ref[0], relation[2 * g + 1], low, slots, at)
    grad = dot3((grad_high[...], grad_low[...]), (high[...], low[...]), NT)
    new_heads, state_out[...] = adagrad(heads[...], state[...], grad)
    heads_out[...] = new_heads
    if not last:
        write_head_parts(me_ref[0], new_heads, outs, *rest[-2:], slots)


def split_kernel(rows, *refs):
    chunks, (high, low) = refs[:-2], refs[-2:]
    at = 0
    for chunk, n in zip(chunks, rows):
        high[at : at + n, :], low[at : at + n, :] = split(chunk[:n, :])
        at += n


def sum_kernel(a, b, *totals):
    at = 0
    for total in totals:
        rows = slice(at, at + total.shape[0])
        total[...] = a[rows, :] + b[rows, :]
        at += total.shape[0]


def total_kernel(place, a, b, c, total):
    rows = slice(place * total.shape[0], (place + 1) * total.shape[0])
    total[...] = a[rows, :] + b[rows, :] + c[...]


def relation_kernel(relation, state, *rest):
    pieces, (relation_out, state_out) = rest[:-2], rest[-2:]
    grad = pieces[0][...]
    for piece in pieces[1:]:
        grad = grad + piece[...]
    relation_out[...], state_out[...] = adagrad(relation[...], state[...], grad)


def call(kernel, outs, args, scratch=(), smem_first=False, flops=0):
    specs = [VMEM] * len(args)
    if smem_first:
        specs[0] = SMEM
    moved = sum(a.size * a.dtype.itemsize for a in args)
    return pl.pallas_call(
        kernel,
        out_shape=[jax.ShapeDtypeStruct(s, t) for s, t in outs],
        in_specs=specs,
        out_specs=[VMEM] * len(outs),
        scratch_shapes=[pltpu.VMEM(s, t) for s, t in scratch],
        compiler_params=pltpu.CompilerParams(vmem_limit_bytes=20 * 1024 * 1024),
        cost_estimate=pl.CostEstimate(flops=flops, bytes_accessed=moved, transcendentals=0),
    )(*args)


def partner(value, mask):
    n = lax.axis_size("blk")
    return lax.ppermute(value, "blk", [(i, i ^ mask) for i in range(n)])


def after(value, *others):
    return lax.optimization_barrier((value, *others))[0]


def gather_groups(own, early, late, use):
    n = lax.axis_size("blk")
    far = list(range(4, n, 4))
    got = {0: own}
    step = n // 2
    while step >= 4:
        for k in [k for k in (0, *far) if k in got]:
            got[k ^ step] = partner(got[k], step)
        if step == n // 2:
            got[2] = partner(own, 2)
            got[step] = after(got[step], *early, *([] if late else [got[2]]))
        step //= 2
    for k in far:
        got[k ^ 2] = partner(got[k], 2)
    waited = late
    for k in (0, *far):
        first = after(got[k], *waited) if k == far[-1] else got[k]
        got[k ^ 1], got[k ^ 3] = partner(first, 1), partner(got[k ^ 2], 1)
        out = use([got[k ^ r] for r in range(4)], k == far[-1])
        if k == 0:
            waited = [*waited, out]
    return out


def pick_slots(n):
    order = (*range(n - 4, 0, -4), 0)
    return [[k ^ r for k in order] for r in (2, 3, 0, 1)]


def scatter_blocks(n, across, across_far, here, here_far):
    order = (*range(n - 4, 0, -4), 0)
    share = across.shape[0] // len(order)
    shape = ((share, across.shape[1]), F32)
    turned = partner(across_far, 1), partner(here_far, 1)
    sent = call(sum_kernel, [shape] * len(order), [across, turned[0]])
    crossed = [partner(value, 2) for value in sent]
    totals = {
        k: call(functools.partial(total_kernel, i), [shape], [here, turned[1], crossed[i]])[0]
        for i, k in enumerate(order)
    }
    step = 4
    while step < n // 2:
        for k in [k for k in totals if k & step]:
            (totals[k ^ step],) = call(sum_kernel, [shape], [totals[k ^ step], partner(totals.pop(k), step)])
        step *= 2
    return [totals[0], partner(totals[step], step)], crossed


def body(heads, head_state, tails, tail_state, relation, relation_state, pos_head, pos_tail):
    share, width = relation.shape
    n = lax.axis_size("blk")
    by_blocks = share % 16 == 0 and n & (n - 1) == 0 and n >= 16
    slots = n if by_blocks else 1
    me = (lax.axis_index("blk").astype(jnp.int32) if by_blocks else jnp.int32(0)).reshape(1)
    head_rows, tail_rows = heads.shape[0], tails.shape[0]
    head_state, tail_state, relation_state = (s.reshape(1, -1) for s in (head_state, tail_state, relation_state))

    def gathered(rows, early, late, use):
        if by_blocks:
            return gather_groups(rows, early, late, use)
        return use([lax.all_gather(rows, "blk", axis=0, tiled=True)], True)

    def scattered(pieces):
        if by_blocks:
            return scatter_blocks(n, *pieces)
        return [lax.psum_scatter(pieces[0], "blk", scatter_dimension=0, tiled=True)], []

    picks = pick_slots(n) if by_blocks else [[0]]
    sizes = [4 * share] * (n // 4) if by_blocks else [width]
    head_parts = [((width, head_rows), BF16)] * 2
    for size in sizes:
        head_parts += [((head_rows, size), BF16)] * 2
    turned = [((width, head_rows), F32)] * 2
    tail_parts = [((tail_rows, width), BF16)] * 2
    relation_parts = [[((size, width), BF16)] * 2 for size in sizes]
    row_parts = [((head_rows, width), BF16)] * 2
    held = [((len(pick) * (width // slots), width), F32) for pick in picks]
    table = ((head_rows, tail_rows), F32)

    head_half = call(
        functools.partial(prepare_heads_kernel, slots), head_parts, [me, heads], scratch=turned, smem_first=True
    )
    *tail_half, marks = call(
        functools.partial(prepare_tails_kernel, head_rows),
        [*tail_parts, ((2, *table[0]), F32)],
        [tails, pos_head, pos_tail],
    )
    rows = [tail_rows // CHUNKS] * CHUNKS
    sent_shapes = [((r + 8 * (i == CHUNKS - 1), width), F32) for i, r in enumerate(rows)]
    calls = ((1,), (0, 2, 3)) if by_blocks else ((0,),)
    for bucket in range(2):
        last = bucket == 1
        before, relation_half = [], []

        def use(blocks, closing):
            first, g = not before, len(relation_half) // 2
            halves, count = head_half[2 + 2 * g : 4 + 2 * g], len(blocks)
            if closing and last:
                out = call(
                    functools.partial(scores_and_grads_kernel, bucket, first, count, [slots, *[picks[c] for c in calls[0]]]),
                    [*relation_parts[g], *row_parts, table, *row_parts, *[held[c] for c in calls[0]]],
                    [*before[-1:], *blocks, *halves, *tail_half, marks, *head_half[:2]],
                    flops=6 * head_rows * width * (width // len(sizes) + 2 * tail_rows),
                )
                relation_half.extend(out[:2])
                return out
            if closing:
                out = call(
                    functools.partial(scores_kernel, bucket, first, count, [] if last else rows),
                    [*relation_parts[g], *row_parts, table, *([] if last else sent_shapes)],
                    [*before[-1:], *blocks, *halves, *tail_half, marks, *([] if last else [tails, tail_state])],
                    flops=6 * head_rows * width * (width // len(sizes) + 2 * tail_rows),
                )
                relation_half.extend(out[:2])
                return out
            out = call(
                functools.partial(product_kernel, first, count),
                [((head_rows, width), F32), *relation_parts[g]],
                [*before[-1:], *blocks, *halves],
                flops=100000000,
            )
            relation_half.extend(out[1:])
            before.append(out[0])
            return out[0]

        out = gathered(relation, head_half, [] if bucket else [*tail_half, marks], use)
        product, grad_scores, sent = out[2:4], out[4], out[5:]
        if not last:
            moves = [(i, (i + 1) % n) for i in range(n)]
            arrived = [lax.ppermute(v, "blk", moves) for v in sent]
        pieces = dict(zip(calls[0], sent[2:])) if last else {}
        grad_product = sent[:2]
        for chosen in calls[len(pieces) > 0 :]:
            wanted = [slots, *[picks[c] for c in chosen]]
            shapes = [held[c] for c in chosen]
            if pieces:
                out = call(
                    functools.partial(relation_term_kernel, wanted), shapes, [*head_half[:2], *grad_product], flops=6 * head_rows * width * width // 2
                )
            else:
                out = call(
                    functools.partial(grads_kernel, wanted),
                    [*row_parts, *shapes],
                    [*head_half[:2], grad_scores, *tail_half],
                    flops=6 * head_rows * width * width // 2,
                )
                grad_product, out = out[:2], out[2:]
            pieces.update(zip(chosen, out))
        pieces = [pieces[c] for c in range(len(picks))]
        terms, crossed = scattered(pieces)
        if last:
            tails, tail_state = call(
                functools.partial(tails_kernel, rows),
                [((tail_rows, width), F32), (tail_state.shape, F32)],
                [after(grad_scores, *crossed[-1:]), *product, *tails],
                flops=6 * head_rows * width * tail_rows,
            )
        else:
            tails = arrived
            tail_half = call(functools.partial(split_kernel, rows), tail_parts, tails)
        out = call(
            functools.partial(heads_kernel, slots, len(sizes), last),
            [(heads.shape, F32), (head_state.shape, F32), *([] if last else head_parts)],
            [me, after(grad_product[0], *(crossed[-1:] if last else arrived)), grad_product[1], *relation_half, heads, head_state],
            scratch=[((width, width), BF16)] * 2 + ([] if last else turned),
            smem_first=True,
        )
        heads, head_state, head_half = out[0], out[1], out[2:]
        relation, relation_state = call(
            relation_kernel,
            [(relation.shape, F32), (relation_state.shape, F32)],
            [relation, relation_state, *terms],
        )
    return (
        heads,
        head_state.reshape(-1),
        tails,
        tail_state.reshape(-1),
        relation,
        relation_state.reshape(-1),
    )


def solution(mesh):
    rows, flat, pairs = P(("grp", "blk"), None), P(("grp", "blk")), P(None, ("grp", "blk"))
    return jax.shard_map(
        body,
        mesh=mesh,
        in_specs=(rows, flat, rows, flat, rows, flat, pairs, pairs),
        out_specs=(rows, flat, rows, flat, rows, flat),
        check_vma=False,
    )
```

```python
import functools

import jax
import jax.numpy as jnp
from jax import lax
from jax.experimental import pallas as pl
from jax.experimental.pallas import tpu as pltpu
from jax.sharding import PartitionSpec as P

F32 = jnp.float32
BF16 = jnp.bfloat16
NN = (((1,), (0,)), ((), ()))
NT = (((1,), (1,)), ((), ()))
VMEM = pl.BlockSpec(memory_space=pltpu.VMEM)
SMEM = pl.BlockSpec(memory_space=pltpu.SMEM)
CHUNKS = 1


def split(x):
    high = x.astype(BF16)
    return high, (x - high.astype(F32)).astype(BF16)


def dot3(a, b, dims):
    (((i,), (j,)), _) = dims
    left = jnp.concatenate([a[1], a[0], a[0]], axis=i)
    right = jnp.concatenate([b[0], b[1], b[0]], axis=j)
    return lax.dot_general(left, right, dims, preferred_element_type=F32)


def diagonal(n):
    return lax.broadcasted_iota(jnp.int32, (n, n), 0) == lax.broadcasted_iota(jnp.int32, (n, n), 1)


def adagrad(param, state_row, grad):
    n = param.shape[0]
    step = 128 if n % 128 == 0 else n
    eye, starts = diagonal(step), range(0, n, step)
    parts = [jnp.sum(jnp.where(eye, state_row[:, i : i + step], 0.0), axis=1, keepdims=True) for i in starts]
    state = jnp.concatenate(parts, axis=0)
    state = state + jnp.sum(grad * grad, axis=1, keepdims=True) * (1.0 / grad.shape[1])
    parts = [jnp.sum(jnp.where(eye, state[i : i + step, :], 0.0), axis=0, keepdims=True) for i in starts]
    back = jnp.concatenate(parts, axis=1)
    return param - grad * (0.1 / jnp.sqrt(state)), back


def to_slots(me, source, target, slots):
    rows = source.shape[0] // slots
    for r in range(slots):
        start = pl.multiple_of((me ^ r) * rows, rows)
        target[r * rows : (r + 1) * rows, :] = source[pl.ds(start, rows), :]


def from_slots(me, source, target, slots, first):
    rows = target.shape[0] // slots
    count = source.shape[0] // rows
    for r in range(count):
        start = pl.multiple_of((me ^ (first + r)) * rows, rows)
        target[pl.ds(start, rows), :] = source[r * rows : (r + 1) * rows, :]
    return first + count


def write_head_parts(me, heads, outs, normal, slotted, slots):
    normal[...] = heads.T
    to_slots(me, normal, slotted, slots)
    outs[0][...], outs[1][...] = split(slotted[...])
    at = 0
    for high, low in zip(outs[2::2], outs[3::2]):
        columns = high.shape[1]
        high[...], low[...] = split(slotted[at : at + columns, :].T)
        at += columns


def prepare_heads_kernel(slots, me_ref, heads, *rest):
    write_head_parts(me_ref[0], heads[...], rest[:-2], *rest[-2:], slots)


def prepare_tails_kernel(head_rows, tails, pos_head, pos_tail, high, low, marks):
    high[...], low[...] = split(tails[...])
    tail_rows, pairs = tails.shape[0], pos_head.shape[1]
    for bucket in range(2):
        in_head = lax.broadcasted_iota(jnp.int32, (head_rows, pairs), 0) == pos_head[bucket : bucket + 1, :]
        in_tail = lax.broadcasted_iota(jnp.int32, (tail_rows, pairs), 0) == pos_tail[bucket : bucket + 1, :]
        marks[bucket] = lax.dot_general(
            jnp.where(in_head, 1.0, 0.0).astype(BF16),
            jnp.where(in_tail, 1.0, 0.0).astype(BF16),
            NT,
            preferred_element_type=F32,
        )


def add_product(blocks, heads, parts):
    rows = blocks[0].shape[0]
    for r, block in enumerate(blocks):
        at = slice(r * rows, (r + 1) * rows)
        parts[0][at, :], parts[1][at, :] = split(block[...])
    return dot3((heads[0][...], heads[1][...]), (parts[0][...], parts[1][...]), NN)


def product_kernel(first, count, *refs):
    before, refs = (None, refs) if first else (refs[0], refs[1:])
    blocks, heads, product, parts = refs[:count], refs[count : count + 2], refs[count + 2], refs[count + 3 :]
    term = add_product(blocks, heads, parts)
    product[...] = term if first else before[...] + term


def scores_kernel(bucket, first, count, rows, *refs):
    before, refs = (None, refs) if first else (refs[0], refs[1:])
    blocks, refs = refs[:count], refs[count:]
    heads, halves, marks, refs = refs[0:2], refs[2:4], refs[4], refs[5:]
    if rows:
        tails, state, refs = refs[0], refs[1], refs[2:]
    relation, product, scores, chunks = refs[0:2], refs[2:4], refs[4], refs[5:]
    whole = add_product(blocks, heads, relation)
    prod = split(whole if first else before[...] + whole)
    product[0][...], product[1][...] = prod
    grad_scores = (jax.nn.sigmoid(dot3(prod, (halves[0][...], halves[1][...]), NT)) - marks[bucket]) * 0.0625
    scores[...] = grad_scores
    if rows:
        grad = dot3(split(grad_scores.T), prod, NN)
        new, new_state = adagrad(tails[...], state[...], grad)
        at = 0
        for chunk, n in zip(chunks, rows):
            chunk[:n, :] = new[at : at + n, :]
            at += n
        chunks[-1][rows[-1] :, :] = jnp.zeros((chunks[-1].shape[0] - rows[-1], new.shape[1]), F32)
        chunks[-1][rows[-1] : rows[-1] + 1, : tails.shape[0]] = new_state


def grads_kernel(picks, turned_high, turned_low, scores, high, low, *refs):
    grad = split(dot3(split(scores[...]), (high[...], low[...]), NN))
    refs[0][...], refs[1][...] = grad
    relation_term_kernel(picks, turned_high, turned_low, *refs)


def relation_term_kernel(picks, turned_high, turned_low, grad_high, grad_low, *pieces):
    rows = turned_high.shape[0] // picks[0]
    grad = grad_high[...], grad_low[...]
    for piece, slots in zip(pieces, picks[1:]):
        high = jnp.concatenate([turned_high[r * rows : (r + 1) * rows, :] for r in slots], axis=0)
        low = jnp.concatenate([turned_low[r * rows : (r + 1) * rows, :] for r in slots], axis=0)
        piece[...] = dot3((high, low), grad, NN)


def scores_and_grads_kernel(bucket, first, count, picks, *refs):
    held = count + (not first)
    inputs, (turned_high, turned_low), outs = refs[: held + 5], refs[held + 5 : held + 7], refs[held + 7 :]
    scores_kernel(bucket, first, count, [], *inputs, *outs[:5])
    grads_kernel(picks, turned_high, turned_low, outs[4], *inputs[held + 2 : held + 4], *outs[5:])


def tails_kernel(rows, grad_scores, product_high, product_low, *refs):
    grad = dot3(split(grad_scores[...].T), (product_high[...], product_low[...]), NN)
    tails, outs = refs[: len(rows)], refs[len(rows) :]
    state = tails[-1][rows[-1] : rows[-1] + 1, : outs[0].shape[0]]
    held = [t[:n, :] for t, n in zip(tails, rows)]
    outs[0][...], outs[1][...] = adagrad(jnp.concatenate(held, axis=0), state, grad)


def heads_kernel(slots, groups, last, me_ref, grad_high, grad_low, *rest):
    relation, (heads, state, heads_out, state_out), rest = rest[: 2 * groups], rest[2 * groups : 2 * groups + 4], rest[2 * groups + 4 :]
    outs, (high, low) = rest[: 2 + 2 * groups], (rest[:2] if last else rest[2 + 2 * groups : 4 + 2 * groups])
    at = 0
    for g in range(groups):
        from_slots(me_ref[0], relation[2 * g], high, slots, at)
        at = from_slots(me_ref[0], relation[2 * g + 1], low, slots, at)
    grad = dot3((grad_high[...], grad_low[...]), (high[...], low[...]), NT)
    new_heads, state_out[...] = adagrad(heads[...], state[...], grad)
    heads_out[...] = new_heads
    if not last:
        write_head_parts(me_ref[0], new_heads, outs, *rest[-2:], slots)


def split_kernel(rows, *refs):
    chunks, (high, low) = refs[:-2], refs[-2:]
    at = 0
    for chunk, n in zip(chunks, rows):
        high[at : at + n, :], low[at : at + n, :] = split(chunk[:n, :])
        at += n


def sum_kernel(a, b, *totals):
    at = 0
    for total in totals:
        rows = slice(at, at + total.shape[0])
        total[...] = a[rows, :] + b[rows, :]
        at += total.shape[0]


def total_kernel(place, a, b, c, total):
    rows = slice(place * total.shape[0], (place + 1) * total.shape[0])
    total[...] = a[rows, :] + b[rows, :] + c[...]


def relation_kernel(relation, state, *rest):
    pieces, (relation_out, state_out) = rest[:-2], rest[-2:]
    grad = pieces[0][...]
    for piece in pieces[1:]:
        grad = grad + piece[...]
    relation_out[...], state_out[...] = adagrad(relation[...], state[...], grad)


def call(kernel, outs, args, scratch=(), smem_first=False, flops=0):
    specs = [VMEM] * len(args)
    if smem_first:
        specs[0] = SMEM
    moved = sum(a.size * a.dtype.itemsize for a in args)
    return pl.pallas_call(
        kernel,
        out_shape=[jax.ShapeDtypeStruct(s, t) for s, t in outs],
        in_specs=specs,
        out_specs=[VMEM] * len(outs),
        scratch_shapes=[pltpu.VMEM(s, t) for s, t in scratch],
        compiler_params=pltpu.CompilerParams(vmem_limit_bytes=20 * 1024 * 1024),
        cost_estimate=pl.CostEstimate(flops=flops, bytes_accessed=moved, transcendentals=0),
    )(*args)


def partner(value, mask):
    n = lax.axis_size("blk")
    return lax.ppermute(value, "blk", [(i, i ^ mask) for i in range(n)])


def after(value, *others):
    return lax.optimization_barrier((value, *others))[0]


def gather_groups(own, early, late, use):
    n = lax.axis_size("blk")
    far = list(range(4, n, 4))
    got = {0: own}
    step = n // 2
    while step >= 4:
        for k in [k for k in (0, *far) if k in got]:
            got[k ^ step] = partner(got[k], step)
        if step == n // 2:
            got[2] = partner(own, 2)
            got[step] = after(got[step], *early, *([] if late else [got[2]]))
        step //= 2
    for k in far:
        got[k ^ 2] = partner(got[k], 2)
    waited = late
    for k in (0, *far):
        first = after(got[k], *waited) if k == far[-1] else got[k]
        got[k ^ 1], got[k ^ 3] = partner(first, 1), partner(got[k ^ 2], 1)
        out = use([got[k ^ r] for r in range(4)], k == far[-1])
        if k == 0:
            waited = [*waited, out]
    return out


def pick_slots(n):
    order = (*range(n - 4, 0, -4), 0)
    return [[k ^ r for k in order] for r in (2, 3, 0, 1)]


def scatter_blocks(n, across, across_far, here, here_far):
    order = (*range(n - 4, 0, -4), 0)
    share = across.shape[0] // len(order)
    shape = ((share, across.shape[1]), F32)
    turned = partner(across_far, 1), partner(here_far, 1)
    sent = call(sum_kernel, [shape] * len(order), [across, turned[0]])
    crossed = [partner(value, 2) for value in sent]
    totals = {
        k: call(functools.partial(total_kernel, i), [shape], [here, turned[1], crossed[i]])[0]
        for i, k in enumerate(order)
    }
    step = 4
    while step < n // 2:
        for k in [k for k in totals if k & step]:
            (totals[k ^ step],) = call(sum_kernel, [shape], [totals[k ^ step], partner(totals.pop(k), step)])
        step *= 2
    return [totals[0], partner(totals[step], step)], crossed


def body(heads, head_state, tails, tail_state, relation, relation_state, pos_head, pos_tail):
    share, width = relation.shape
    n = lax.axis_size("blk")
    by_blocks = share % 16 == 0 and n & (n - 1) == 0 and n >= 16
    slots = n if by_blocks else 1
    me = (lax.axis_index("blk").astype(jnp.int32) if by_blocks else jnp.int32(0)).reshape(1)
    head_rows, tail_rows = heads.shape[0], tails.shape[0]
    head_state, tail_state, relation_state = (s.reshape(1, -1) for s in (head_state, tail_state, relation_state))

    def gathered(rows, early, late, use):
        if by_blocks:
            return gather_groups(rows, early, late, use)
        return use([lax.all_gather(rows, "blk", axis=0, tiled=True)], True)

    def scattered(pieces):
        if by_blocks:
            return scatter_blocks(n, *pieces)
        return [lax.psum_scatter(pieces[0], "blk", scatter_dimension=0, tiled=True)], []

    picks = pick_slots(n) if by_blocks else [[0]]
    sizes = [4 * share] * (n // 4) if by_blocks else [width]
    head_parts = [((width, head_rows), BF16)] * 2
    for size in sizes:
        head_parts += [((head_rows, size), BF16)] * 2
    turned = [((width, head_rows), F32)] * 2
    tail_parts = [((tail_rows, width), BF16)] * 2
    relation_parts = [[((size, width), BF16)] * 2 for size in sizes]
    row_parts = [((head_rows, width), BF16)] * 2
    held = [((len(pick) * (width // slots), width), F32) for pick in picks]
    table = ((head_rows, tail_rows), F32)

    head_half = call(
        functools.partial(prepare_heads_kernel, slots), head_parts, [me, heads], scratch=turned, smem_first=True
    )
    *tail_half, marks = call(
        functools.partial(prepare_tails_kernel, head_rows),
        [*tail_parts, ((2, *table[0]), F32)],
        [tails, pos_head, pos_tail],
    )
    rows = [tail_rows // CHUNKS] * CHUNKS
    sent_shapes = [((r + 8 * (i == CHUNKS - 1), width), F32) for i, r in enumerate(rows)]
    calls = ((1,), (0, 2, 3)) if by_blocks else ((0,),)
    for bucket in range(2):
        last = bucket == 1
        before, relation_half = [], []

        def use(blocks, closing):
            first, g = not before, len(relation_half) // 2
            halves, count = head_half[2 + 2 * g : 4 + 2 * g], len(blocks)
            if closing and last:
                out = call(
                    functools.partial(scores_and_grads_kernel, bucket, first, count, [slots, *[picks[c] for c in calls[0]]]),
                    [*relation_parts[g], *row_parts, table, *row_parts, *[held[c] for c in calls[0]]],
                    [*before[-1:], *blocks, *halves, *tail_half, marks, *head_half[:2]],
                    flops=6 * head_rows * width * (width // len(sizes) + 2 * tail_rows),
                )
                relation_half.extend(out[:2])
                return out
            if closing:
                out = call(
                    functools.partial(scores_kernel, bucket, first, count, [] if last else rows),
                    [*relation_parts[g], *row_parts, table, *([] if last else sent_shapes)],
                    [*before[-1:], *blocks, *halves, *tail_half, marks, *([] if last else [tails, tail_state])],
                    flops=6 * head_rows * width * (width // len(sizes) + 2 * tail_rows),
                )
                relation_half.extend(out[:2])
                return out
            out = call(
                functools.partial(product_kernel, first, count),
                [((head_rows, width), F32), *relation_parts[g]],
                [*before[-1:], *blocks, *halves],
                flops=100000000,
            )
            relation_half.extend(out[1:])
            before.append(out[0])
            return out[0]

        out = gathered(relation, head_half, [] if bucket else [*tail_half, marks], use)
        product, grad_scores, sent = out[2:4], out[4], out[5:]
        if not last:
            moves = [(i, (i + 1) % n) for i in range(n)]
            arrived = [lax.ppermute(v, "blk", moves) for v in sent]
        pieces = dict(zip(calls[0], sent[2:])) if last else {}
        grad_product = sent[:2]
        for chosen in calls[len(pieces) > 0 :]:
            wanted = [slots, *[picks[c] for c in chosen]]
            shapes = [held[c] for c in chosen]
            if pieces:
                out = call(
                    functools.partial(relation_term_kernel, wanted), shapes, [*head_half[:2], *grad_product], flops=6 * head_rows * width * width // 2
                )
            else:
                out = call(
                    functools.partial(grads_kernel, wanted),
                    [*row_parts, *shapes],
                    [*head_half[:2], grad_scores, *tail_half],
                    flops=6 * head_rows * width * width // 2,
                )
                grad_product, out = out[:2], out[2:]
            pieces.update(zip(chosen, out))
        pieces = [pieces[c] for c in range(len(picks))]
        terms, crossed = scattered(pieces)
        if last:
            tails, tail_state = call(
                functools.partial(tails_kernel, rows),
                [((tail_rows, width), F32), (tail_state.shape, F32)],
                [after(grad_scores, *crossed[-1:]), *product, *tails],
                flops=6 * head_rows * width * tail_rows,
            )
        else:
            tails = arrived
            tail_half = call(functools.partial(split_kernel, rows), tail_parts, tails)
        out = call(
            functools.partial(heads_kernel, slots, len(sizes), last),
            [(heads.shape, F32), (head_state.shape, F32), *([] if last else head_parts)],
            [me, after(grad_product[0], *(crossed[-1:] if last else arrived)), grad_product[1], *relation_half, heads, head_state],
            scratch=[((width, width), BF16)] * 2 + ([] if last else turned),
            smem_first=True,
        )
        heads, head_state, head_half = out[0], out[1], out[2:]
        relation, relation_state = call(
            relation_kernel,
            [(relation.shape, F32), (relation_state.shape, F32)],
            [relation, relation_state, *terms],
        )
    return (
        heads,
        head_state.reshape(-1),
        tails,
        tail_state.reshape(-1),
        relation,
        relation_state.reshape(-1),
    )


def solution(mesh):
    rows, flat, pairs = P(("grp", "blk"), None), P(("grp", "blk")), P(None, ("grp", "blk"))
    return jax.shard_map(
        body,
        mesh=mesh,
        in_specs=(rows, flat, rows, flat, rows, flat, pairs, pairs),
        out_specs=(rows, flat, rows, flat, rows, flat),
        check_vma=False,
    )
```
